128 devices in a mesh: row: 8 (over y, x_hi), col: 16 (over z, x_lo, core).
Axes of the slice: x: 4 (x_hi: 2, x_lo: 2; x = x_hi * 2 + x_lo), y: 4, z: 4, core: 2. Of those that a mesh axis runs over, the one named last changes fastest.
Arguments:
- teacher: bfloat16 [16384, 256], replicated, may hold values from -4 to 4
- panel_ids: int32 [2048], P('col'), may hold values from 0 to 16383
- rest_ids: int32 [8, 16, 128], P('row', 'col'), may hold values from 0 to 16383
- inverse: bfloat16 [2048, 2048], replicated, may hold values from -1 to 1, as said below
Outputs:
- trailing: float32 [16, 8, 128, 8, 16, 128], P(None, 'row', None, None, 'col')
- panel_rows: bfloat16 [8, 16, 128, 2048], P('row', 'col')
The draws below stay inside these ranges and needn't reach their ends.
Inputs may be any that keep to these rules, and one draw needn't show every extreme that they name: `inverse`: zero above the diagonal.
All inputs are finite; a program needn't handle non-finite values.
Results may differ from the reference program's by a relative error of at most 0.0049.
Values may be sent and summed in bfloat16 or wider, within the bound.
No kernel may reach another device: no remote copies, remote signals or barrier semaphores. Data moves between devices by JAX's collectives and lax.ppermute only.
A program may use at most 128 MiB of HBM per device.

```python
import math
import jax
import jax.numpy as jnp
from jax import lax

E = 256
P_SIZE = 2048
VOCAB = 16384
STRETCH = 128
N_ROW = 8
N_COL = 16


def draw_teacher(key, part):
    first_key, second_key = jax.random.split(key, 2)
    groups = 16
    repeats = E // groups
    coords = jnp.clip(jax.random.normal(first_key, (VOCAB, groups), jnp.float32) * math.sqrt(0.5), -3.0, 3.0)
    noise = jnp.clip(0.2 * jax.random.normal(second_key, (VOCAB, E), jnp.float32), -0.8, 0.8)
    tiled = jnp.broadcast_to(coords[:, None, :], (VOCAB, repeats, groups)).reshape(VOCAB, E)
    return jnp.clip(tiled + noise, -4.0, 4.0).astype(jnp.bfloat16)


def draw_inverse(key, part):
    first_key, second_key = jax.random.split(key, 2)
    diagonal = jnp.exp(jax.random.uniform(first_key, (P_SIZE,), jnp.float32, math.log(0.5), math.log(2.0)))
    offdiag = jnp.clip(jax.random.normal(second_key, (P_SIZE, P_SIZE), jnp.float32), -4.0, 4.0)
    places = jnp.arange(P_SIZE)
    lower = places[:, None] > places[None, :]
    matrix = jnp.where(lower, offdiag / math.sqrt(P_SIZE), 0.0) + jnp.diag(diagonal)
    return (matrix * (5.0 / math.sqrt(P_SIZE))).astype(jnp.bfloat16)


def plant(values, rng, low, largest):
    place = [jax.random.randint(jax.random.fold_in(rng, axis), (), 0, length) for axis, length in enumerate(values.shape)]
    main_axis = values.shape.index(max(values.shape))
    neighbour = place[:main_axis] + [(place[main_axis] + 1) % values.shape[main_axis]] + place[main_axis + 1:]
    return values.at[tuple(place)].set(low).at[tuple(neighbour)].set(largest)


def setup_inputs(seed: int = 0) -> dict:
    splits = jax.random.split(jax.random.key(seed), 5)
    teacher = draw_teacher(jax.random.fold_in(splits[4], 71), 0)
    panel_ids = plant(jax.random.randint(splits[1], (P_SIZE,), 0, VOCAB), jax.random.fold_in(splits[1], 1), 0, VOCAB - 1).astype(jnp.int32)
    rest_ids = plant(jax.random.randint(splits[2], (N_ROW, N_COL, STRETCH), 0, VOCAB), jax.random.fold_in(splits[2], 1), 0, VOCAB - 1).astype(jnp.int32)
    inverse = draw_inverse(jax.random.fold_in(splits[4], 71), 0)
    return {"teacher": teacher, "panel_ids": panel_ids, "rest_ids": rest_ids, "inverse": inverse}


def gaussian(left_rows, right_rows, inv_scale):
    sq_left = jnp.sum(jnp.square(left_rows.astype(jnp.float32)), axis=-1)
    sq_right = jnp.sum(jnp.square(right_rows.astype(jnp.float32)), axis=-1)
    inner = lax.dot_general(left_rows, right_rows, (((1,), (1,)), ((), ())), preferred_element_type=jnp.float32)
    return jnp.exp(-inv_scale * (sq_left[:, None] + sq_right[None, :] - 2.0 * inner))


def reference(teacher, panel_ids, rest_ids, inverse):
    inv_scale = 2.0 / E
    panel_emb = teacher[panel_ids]
    rest_emb = teacher[rest_ids.reshape(-1)]
    kernel = gaussian(rest_emb, panel_emb, inv_scale).astype(jnp.bfloat16)
    factors = lax.dot_general(kernel, inverse, (((1,), (1,)), ((), ())), preferred_element_type=jnp.float32).astype(jnp.bfloat16)
    total = rest_emb.shape[0]
    span = total // N_COL

    def one_block(block_at):
        first_row = block_at * span
        left_emb = lax.dynamic_slice_in_dim(rest_emb, first_row, span, 0)
        left_factor = lax.dynamic_slice_in_dim(factors, first_row, span, 0)
        update = lax.dot_general(left_factor, factors, (((1,), (1,)), ((), ())), preferred_element_type=jnp.float32)
        result = gaussian(left_emb, rest_emb, inv_scale) - update
        row_index = first_row + jnp.arange(span, dtype=jnp.int32)
        col_index = jnp.arange(total, dtype=jnp.int32)
        return jnp.where(row_index[:, None] >= col_index[None, :], result, jnp.zeros_like(result))

    full = lax.map(one_block, jnp.arange(N_COL, dtype=jnp.int32))
    trailing = full.reshape(N_COL, N_ROW, STRETCH, N_ROW, N_COL, STRETCH)
    return trailing, factors.reshape(N_ROW, N_COL, STRETCH, P_SIZE)
```

```python
import jax
import jax.numpy as jnp
from jax import lax
from jax.sharding import PartitionSpec as P


def sq_norms(rows):
    return jnp.sum(jnp.square(rows.astype(jnp.float32)), axis=-1)


def gaussian(left_rows, right_rows, inv_scale):
    inner = lax.dot_general(
        left_rows, right_rows, (((1,), (1,)), ((), ())), preferred_element_type=jnp.float32
    )
    return jnp.exp(
        -inv_scale * (sq_norms(left_rows)[:, None] + sq_norms(right_rows)[None, :] - 2.0 * inner)
    )


def factor(kernel, inverse):
    n_blocks = 4
    block_width = inverse.shape[0] // n_blocks
    pieces = []
    for block_at in range(n_blocks):
        finish = (block_at + 1) * block_width
        pieces.append(
            lax.dot_general(
                kernel[:, :finish],
                inverse[block_at * block_width : finish, :finish],
                (((1,), (1,)), ((), ())),
                preferred_element_type=jnp.float32,
            ).astype(jnp.bfloat16)
        )
    return jnp.concatenate(pieces, 1)


def shards(teacher, panel_ids, rest_ids, inverse):
    n_row = lax.axis_size("row")
    n_col = lax.axis_size("col")
    row_at = lax.axis_index("row")
    col_at = lax.axis_index("col")
    stretch_rows = rest_ids.shape[2]
    inv_scale = 2.0 / teacher.shape[1]
    both = jnp.concatenate([rest_ids.reshape(1, -1), panel_ids.reshape(1, -1)], 0)
    both = jnp.broadcast_to(both[None], (n_row * n_col, *both.shape))
    both = lax.all_to_all(both, ("row", "col"), 0, 0, tiled=True)
    panel = both[:n_col, 1].reshape(-1)
    blocks = both[:, 0]
    col_ids = lax.dynamic_index_in_dim(
        blocks.reshape(n_row, n_col, stretch_rows), col_at, 1, False
    ).reshape(-1)
    row_ids = lax.dynamic_index_in_dim(
        blocks.reshape(n_col, n_row, stretch_rows), row_at, 1, False
    ).reshape(-1)
    n_col_ids, n_row_ids = col_ids.shape[0], row_ids.shape[0]
    emb = teacher[jnp.concatenate([col_ids, row_ids, panel])]
    x_emb = emb[: n_col_ids + n_row_ids]
    panel_emb = emb[n_col_ids + n_row_ids :]
    col_emb, row_emb = x_emb[:n_col_ids], x_emb[n_col_ids:]
    cross = gaussian(x_emb, panel_emb, inv_scale).astype(jnp.bfloat16)
    factors = factor(cross, inverse)
    col_factor, row_factor = factors[:n_col_ids], factors[n_col_ids:]
    own_factor = lax.dynamic_slice_in_dim(col_factor, row_at * stretch_rows, stretch_rows, 0)
    update = lax.dot_general(
        row_factor, col_factor, (((1,), (1,)), ((), ())), preferred_element_type=jnp.float32
    )
    rows_local = jnp.arange(n_col * stretch_rows, dtype=jnp.int32)
    row_index = (
        rows_local // stretch_rows * n_row + row_at
    ) * stretch_rows + rows_local % stretch_rows
    cols_local = jnp.arange(n_row * stretch_rows, dtype=jnp.int32)
    col_index = (
        cols_local // stretch_rows * n_col + col_at
    ) * stretch_rows + cols_local % stretch_rows
    result = gaussian(row_emb, col_emb, inv_scale) - update
    trailing = jnp.where(row_index[:, None] >= col_index[None, :], result, jnp.zeros_like(result))
    return (
        trailing.reshape(n_col, 1, stretch_rows, n_row, 1, stretch_rows),
        own_factor.reshape(1, 1, stretch_rows, own_factor.shape[1]),
    )


def solution(mesh):
    return jax.shard_map(
        shards,
        mesh=mesh,
        in_specs=(P(), P("col"), P("row", "col", None), P()),
        out_specs=(P(None, "row", None, None, "col", None), P("row", "col", None, None)),
        check_vma=False,
    )
```

```python
import functools
import math

import jax
import jax.numpy as jnp
from jax import lax
from jax.experimental import pallas as pl
from jax.experimental.pallas import tpu as pltpu
from jax.sharding import PartitionSpec as P

BF16, F32 = jnp.bfloat16, jnp.float32
MIB = 1 << 20
LANES = 128
CHUNK = 512
WIDE = 256


def nt_dot(left, right):
    return lax.dot_general(left, right, (((1,), (1,)), ((), ())), preferred_element_type=F32)


def column_norms(rows, scale):
    wide = rows.astype(F32)
    return scale * jnp.sum(wide * wide, axis=1, keepdims=True)


def lane_norms(rows, scale):
    wide = rows.astype(F32)
    square = wide * wide
    high = square.astype(BF16)
    low = (square - high.astype(F32)).astype(BF16)
    ones = jnp.ones((8, rows.shape[1]), BF16)
    return scale * (nt_dot(ones, high) + nt_dot(ones, low))


def split_kernel(scale, n_sets, teacher_ref, panel_ids, row_ids, col_ids, inverse_ref,
                 factor_out, panel_out, norm_out, row_out, col_out,
                 left, right, stage_left, stage_right, cross, ids, sems):
    row_at, col_at = lax.axis_index("row"), lax.axis_index("col")
    n_panel, n_rows, n_cols = n_sets
    copies = [
        pltpu.make_async_copy(panel_ids.at[pl.ds(0, n_panel), 1], ids.at[pl.ds(0, n_panel)], sems.at[0]),
        pltpu.make_async_copy(row_ids.at[:, row_at, 0], ids.at[pl.ds(n_panel, n_rows)], sems.at[1]),
        pltpu.make_async_copy(col_ids.at[:, col_at, 0], ids.at[pl.ds(n_panel + n_rows, n_cols)], sems.at[2]),
    ]
    for copy in copies:
        copy.start()

    def widen(step, carry):
        at = pl.ds(pl.multiple_of(step * CHUNK, CHUNK), CHUNK)
        left[at, :] = teacher_ref[at, :LANES].astype(F32)
        right[at, :] = teacher_ref[at, LANES:].astype(F32)
        return carry

    lax.fori_loop(0, teacher_ref.shape[0] // CHUNK, widen, 0)
    for copy in copies:
        copy.wait()

    stretch = ids.shape[2]

    def gather(first_block, out):
        def chunk(step, carry):
            def some(part, carry):
                for u in range(32):
                    at = part * 32 + u
                    row = ids[first_block + step * (CHUNK // stretch) + part // (stretch // 32), 0,
                              (part % (stretch // 32)) * 32 + u]
                    stage_left[pl.ds(at, 1), :] = left[pl.ds(row, 1), :]
                    stage_right[pl.ds(at, 1), :] = right[pl.ds(row, 1), :]
                return carry

            lax.fori_loop(0, CHUNK // 32, some, 0)
            to = pl.ds(pl.multiple_of(step * CHUNK, CHUNK), CHUNK)
            out[to, :LANES] = stage_left[...].astype(BF16)
            out[to, LANES:] = stage_right[...].astype(BF16)
            return carry

        lax.fori_loop(0, out.shape[0] // CHUNK, chunk, 0)

    gather(0, panel_out)
    for at in range(0, panel_out.shape[0], CHUNK):
        norm_out[:, at : at + CHUNK] = lane_norms(panel_out[at : at + CHUNK, :], scale)
    gather(n_panel, row_out)
    half = factor_out.shape[0]
    mine = pl.multiple_of(col_at % 2 * half, half)
    factor_rows(scale, row_out[pl.ds(mine, half), :], panel_out, norm_out, inverse_ref, cross, factor_out)
    gather(n_panel + n_rows, col_out)


def factor_rows(scale, rows, panel_ref, norm_ref, inverse_ref, cross, factor_ref):
    norms = column_norms(rows, scale)
    for at in range(0, panel_ref.shape[0], WIDE):
        to = slice(at, at + WIDE)
        inner = nt_dot(rows, panel_ref[to, :])
        cross[:, to] = jnp.exp2(2.0 * scale * inner - norms - norm_ref[:1, to]).astype(BF16)
        factor_ref[:, to] = nt_dot(cross[:, : at + WIDE], inverse_ref[to, : at + WIDE]).astype(BF16)


def column_kernel(scale, stretch, col_ref, panel_ref, norm_ref, inverse_ref, factor_out, own_out, cross, sem):
    factor_rows(scale, col_ref[...], panel_ref, norm_ref, inverse_ref, cross, factor_out)
    own = pl.ds(pl.multiple_of(lax.axis_index("row") * stretch, stretch), stretch)
    copy = pltpu.make_async_copy(factor_out.at[own], own_out, sem)
    copy.start()
    copy.wait()


def update_kernel(scale, n_row, n_col, stretch, mine_hbm, other_hbm, factor_ref, row_ref, col_ref, out_hbm,
                  rows, stage, norms, in_sems, out_sems):
    row_at, col_at = lax.axis_index("row"), lax.axis_index("col")
    tile = rows.shape[1]
    n_tiles = row_ref.shape[0] // tile
    half_tiles = mine_hbm.shape[0] // tile
    parity = col_at % 2
    for at in range(0, col_ref.shape[0], CHUNK):
        norms[:, at : at + CHUNK] = lane_norms(col_ref[at : at + CHUNK, :], scale)

    def fetch(m, slot):
        src = pl.ds(pl.multiple_of(m % half_tiles * tile, tile), tile)

        @pl.when(m // half_tiles == parity)
        def _():
            pltpu.make_async_copy(mine_hbm.at[src], rows.at[slot], in_sems.at[slot]).start()

        @pl.when(m // half_tiles != parity)
        def _():
            pltpu.make_async_copy(other_hbm.at[src], rows.at[slot], in_sems.at[slot]).start()

    def put(m, slot):
        size = stage.shape[1]
        return pltpu.make_async_copy(
            stage.at[slot], out_hbm.at[pl.ds(pl.multiple_of(m * size, size), size)], out_sems.at[slot])

    fetch(n_tiles - 1, 0)
    above = lax.broadcasted_iota(jnp.int32, (tile, LANES), 0)
    above = above // stretch * (n_row * stretch) + above % stretch - lax.broadcasted_iota(jnp.int32, (tile, LANES), 1)

    def one_tile(step, carry):
        m = n_tiles - 1 - step
        slot = step % 2

        @pl.when(step + 1 < n_tiles)
        def _():
            fetch(m - 1, 1 - slot)

        @pl.when(step >= 2)
        def _():
            put(m + 2, slot).wait()

        pltpu.make_async_copy(mine_hbm.at[pl.ds(0, tile)], rows.at[slot], in_sems.at[slot]).wait()
        rows_emb = row_ref[pl.ds(pl.multiple_of(m * tile, tile), tile), :]
        row_norms = column_norms(rows_emb, scale)
        first_row = (m * (tile // stretch) * n_row + row_at) * stretch

        for n in range(factor_ref.shape[0] // WIDE):
            blocks = [(n * (WIDE // LANES) + b) for b in range(WIDE // LANES)]

            @pl.when(n <= m)
            def _():
                to = slice(n * WIDE, (n + 1) * WIDE)
                update = nt_dot(rows[slot], factor_ref[to, :])
                inner = nt_dot(rows_emb, col_ref[to, :])
                result = jnp.exp2(2.0 * scale * inner - row_norms - norms[:1, to]) - update
                for b, block in enumerate(blocks):
                    first_col = (block * n_col + col_at) * stretch
                    piece = result[:, b * LANES : (b + 1) * LANES]
                    piece = jnp.where(above >= first_col - first_row, piece, 0.0)
                    stage[slot, pl.ds(block, tile, stride=n_row), :] = piece

            @pl.when(n > m)
            def _():
                for block in blocks:
                    stage[slot, pl.ds(block, tile, stride=n_row), :] = jnp.zeros((tile, LANES), F32)

        put(m, slot).start()
        return carry

    lax.fori_loop(0, n_tiles, one_tile, 0)
    put(1, (n_tiles - 2) % 2).wait()
    put(0, (n_tiles - 1) % 2).wait()


def shards(teacher, panel_ids, rest_ids, inverse):
    n_row, n_col = lax.axis_size("row"), lax.axis_size("col")
    stretch = rest_ids.shape[2]
    width = inverse.shape[0]
    n_rows, n_cols = n_col * stretch, n_row * stretch
    half = n_rows // 2
    scale = 2.0 / teacher.shape[1] * math.log2(math.e)
    vmem = pl.BlockSpec(memory_space=pltpu.VMEM)
    hbm = pl.BlockSpec(memory_space=pl.ANY)
    both = jnp.concatenate([rest_ids.reshape(1, 1, -1), panel_ids.reshape(1, 1, -1)], 0)
    both = jnp.broadcast_to(both[None], (n_row * n_col, *both.shape))
    both = lax.all_to_all(both, ("row", "col"), 0, 0, tiled=True)

    mine, panel_emb, panel_norms, row_emb, col_emb = pl.pallas_call(
        functools.partial(split_kernel, scale, (n_col, n_col, n_row)),
        out_shape=(
            jax.ShapeDtypeStruct((half, width), BF16),
            jax.ShapeDtypeStruct((width, teacher.shape[1]), BF16),
            jax.ShapeDtypeStruct((8, width), F32),
            jax.ShapeDtypeStruct((n_rows, teacher.shape[1]), BF16),
            jax.ShapeDtypeStruct((n_cols, teacher.shape[1]), BF16),
        ),
        in_specs=[vmem, hbm, hbm, hbm, vmem],
        out_specs=[vmem] * 5,
        scratch_shapes=[
            pltpu.VMEM((teacher.shape[0], LANES), F32),
            pltpu.VMEM((teacher.shape[0], LANES), F32),
            pltpu.VMEM((CHUNK, LANES), F32),
            pltpu.VMEM((CHUNK, LANES), F32),
            pltpu.VMEM((half, width), BF16),
            pltpu.SMEM((2 * n_col + n_row, 1, stretch), jnp.int32),
            pltpu.SemaphoreType.DMA((3,)),
        ],
        compiler_params=pltpu.CompilerParams(vmem_limit_bytes=56 * MIB),
        name="rows",
    )(teacher, both, both.reshape(n_col, n_row, 2, 1, stretch), both.reshape(n_row, n_col, 2, 1, stretch), inverse)

    other = lax.ppermute(mine, "col", [(i, i ^ 1) for i in range(n_col)])

    factors, own = pl.pallas_call(
        functools.partial(column_kernel, scale, stretch),
        out_shape=(
            jax.ShapeDtypeStruct((n_cols, width), BF16),
            jax.ShapeDtypeStruct((stretch, width), BF16),
        ),
        in_specs=[vmem] * 4,
        out_specs=[vmem, hbm],
        scratch_shapes=[pltpu.VMEM((n_cols, width), BF16), pltpu.SemaphoreType.DMA],
        compiler_params=pltpu.CompilerParams(vmem_limit_bytes=32 * MIB),
        cost_estimate=pl.CostEstimate(
            flops=2 * n_cols * width * width, bytes_accessed=16 * MIB, transcendentals=n_cols * width),
        name="columns",
    )(col_emb, panel_emb, panel_norms, inverse)

    tile = 4 * stretch
    trailing = pl.pallas_call(
        functools.partial(update_kernel, scale, n_row, n_col, stretch),
        out_shape=jax.ShapeDtypeStruct((n_rows * n_row, stretch), F32),
        in_specs=[hbm, hbm, vmem, vmem, vmem],
        out_specs=hbm,
        scratch_shapes=[
            pltpu.VMEM((2, tile, width), BF16),
            pltpu.VMEM((2, tile * n_row, stretch), F32),
            pltpu.VMEM((8, n_cols), F32),
            pltpu.SemaphoreType.DMA((2,)),
            pltpu.SemaphoreType.DMA((2,)),
        ],
        compiler_params=pltpu.CompilerParams(vmem_limit_bytes=32 * MIB),
        name="update",
    )(mine, other, factors, row_emb, col_emb)
    return (
        trailing.reshape(n_col, 1, stretch, n_row, 1, stretch),
        own.reshape(1, 1, stretch, width),
    )


def solution(mesh):
    return jax.shard_map(
        shards,
        mesh=mesh,
        in_specs=(P(), P("col"), P("row", "col", None), P()),
        out_specs=(P(None, "row", None, None, "col", None), P("row", "col", None, None)),
        check_vma=False,
    )
```

```python
import functools
import math

import jax
import jax.numpy as jnp
from jax import lax
from jax.experimental import pallas as pl
from jax.experimental.pallas import tpu as pltpu
from jax.sharding import PartitionSpec as P

BF16, F32 = jnp.bfloat16, jnp.float32
MIB = 1 << 20
LANES = 128
WIDE = 256
PIECE = 1024


def nt_dot(left, right):
    return lax.dot_general(left, right, (((1,), (1,)), ((), ())), preferred_element_type=F32)


def split_squares(rows):
    wide = rows.astype(F32)
    square = wide * wide
    high = square.astype(BF16)
    return high, (square - high.astype(F32)).astype(BF16)


def row_norms(rows, scale):
    high, low = split_squares(rows)
    ones = jnp.ones((LANES, rows.shape[1]), BF16)
    return scale * (nt_dot(high, ones) + nt_dot(low, ones))


def lane_norms(rows, scale):
    high, low = split_squares(rows)
    ones = jnp.ones((8, rows.shape[1]), BF16)
    return scale * (nt_dot(ones, high) + nt_dot(ones, low))


def gauss(scale, inner, norms, other_norms):
    norms = jnp.concatenate([norms] * (inner.shape[1] // LANES), 1)
    return jnp.exp2(2.0 * scale * inner - norms - other_norms)


def start_load(teacher, inverse, inverse_out, pieces, sems, inverse_sems):
    copies = [
        pltpu.make_async_copy(teacher.at[pl.ds(i * PIECE, PIECE)], pieces.at[i], sems.at[i])
        for i in range(pieces.shape[0])
    ]
    inverse_copies = []
    for i in range(inverse.shape[0] // WIDE):
        at = (pl.ds(i * WIDE, WIDE), pl.ds(0, (i + 1) * WIDE))
        inverse_copies.append(pltpu.make_async_copy(inverse.at[at], inverse_out.at[at], inverse_sems.at[i]))
    for copy in copies + inverse_copies:
        copy.start()
    return copies, inverse_copies


def widen(copies, pieces, left, right):
    for i, copy in enumerate(copies):
        copy.wait()

        def step(part, carry):
            at = pl.ds(pl.multiple_of(part * WIDE, WIDE), WIDE)
            to = pl.ds(pl.multiple_of(i * PIECE + part * WIDE, WIDE), WIDE)
            left[to, :] = pieces[i, at, :LANES].astype(F32)
            right[to, :] = pieces[i, at, LANES:].astype(F32)
            return carry

        lax.fori_loop(0, PIECE // WIDE, step, 0)


def rows_kernel(scale, n_sets, teacher, inverse, panel_ids, row_ids, col_ids,
                half_out, panel_out, norm_out, col_out, inverse_ref,
                pieces, left, right, stage_left, stage_right, norms, cross, ids, sems, piece_sems, inverse_sems):
    row_at, col_at = lax.axis_index("row"), lax.axis_index("col")
    n_panel, n_rows, n_cols = n_sets
    copies = [
        pltpu.make_async_copy(panel_ids.at[pl.ds(0, n_panel), 1], ids.at[pl.ds(0, n_panel)], sems.at[0]),
        pltpu.make_async_copy(row_ids.at[:, row_at, 0], ids.at[pl.ds(n_panel, n_rows)], sems.at[1]),
        pltpu.make_async_copy(col_ids.at[:, col_at, 0], ids.at[pl.ds(n_panel + n_rows, n_cols)], sems.at[2]),
    ]
    for copy in copies:
        copy.start()
    piece_copies, inverse_copies = start_load(teacher, inverse, inverse_ref, pieces, piece_sems, inverse_sems)
    widen(piece_copies, pieces, left, right)
    for copy in copies:
        copy.wait()
    stretch = ids.shape[2]
    width = panel_out.shape[0]

    def gather(id_block, out, at, column, slot):
        for u in range(stretch):
            row = ids[id_block, 0, u]
            stage_left[slot, u : u + 1, :] = left[pl.ds(row, 1), :]
            stage_right[slot, u : u + 1, :] = right[pl.ds(row, 1), :]
        to = pl.ds(pl.multiple_of(at, stretch), stretch)
        out[to, column : column + LANES] = stage_left[slot].astype(BF16)
        out[to, column + LANES : column + 2 * LANES] = stage_right[slot].astype(BF16)

    def gather_pairs(id_pair, count, out, column):
        def one(i, carry):
            for b in range(2):
                gather(id_pair(i) + b, out, (2 * i + b) * stretch, column, b)
            return carry

        lax.fori_loop(0, count // 2, one, 0)

    gather_pairs(lambda i: n_panel + 4 * i + 2 * (col_at % 2), n_rows // 2, half_out, width)
    gather_pairs(lambda i: 2 * i, n_panel, panel_out, 0)
    gather_pairs(lambda i: n_panel + n_rows + 2 * i, n_cols, col_out, 0)
    norms[...] = row_norms(half_out[:, width:], scale)
    for at in range(0, width, WIDE):
        norm_out[:, at : at + WIDE] = lane_norms(panel_out[at : at + WIDE, :], scale)
    for copy in inverse_copies:
        copy.wait()
    cross_rows(scale, lambda: half_out[:, width:], norms, panel_out, norm_out, cross)
    for j in range(width // WIDE):
        factor_columns(j, inverse_ref, cross, half_out)


def cross_rows(scale, rows, norms, panel_ref, norm_ref, cross):
    for at in range(0, panel_ref.shape[0], WIDE):
        to = slice(at, at + WIDE)
        cross[:, to] = gauss(scale, nt_dot(rows(), panel_ref[to, :]), norms[...], norm_ref[:1, to]).astype(BF16)


def factor_columns(j, inverse_ref, cross, factor_ref):
    to, depth = slice(j * WIDE, (j + 1) * WIDE), (j + 1) * WIDE
    factor_ref[:, to] = nt_dot(cross[:, :depth], inverse_ref[to, :depth]).astype(BF16)


def column_kernel(scale, stretch, col_ref, panel_ref, norm_ref, inverse_ref, factor_out, own_out, norms, cross, sems):
    norms[...] = row_norms(col_ref[...], scale)
    cross_rows(scale, lambda: col_ref[...], norms, panel_ref, norm_ref, cross)
    own = pl.ds(pl.multiple_of(lax.axis_index("row") * stretch, stretch), stretch)
    n_steps = panel_ref.shape[0] // WIDE
    copies = []
    for j in range(n_steps):
        factor_columns(j, inverse_ref, cross, factor_out)
        to = pl.ds(j * WIDE, WIDE)
        copies.append(pltpu.make_async_copy(factor_out.at[own, to], own_out.at[:, to], sems.at[j]))
        copies[-1].start()
    for copy in copies:
        copy.wait()


def update_kernel(scale, n_row, n_col, stretch, mine, other, factor_ref, col_ref, out_hbm,
                  stage, norms, row_norm, out_sems):
    row_at, col_at = lax.axis_index("row"), lax.axis_index("col")
    parity = col_at % 2
    width = factor_ref.shape[1]
    tile = 2 * stretch
    n_cols = factor_ref.shape[0]
    for at in range(0, n_cols, WIDE):
        norms[:, at : at + WIDE] = lane_norms(col_ref[at : at + WIDE, :], scale)
    above = lax.broadcasted_iota(jnp.int32, (tile, LANES), 0)
    above = above // stretch * (n_row * stretch) + above % stretch - lax.broadcasted_iota(jnp.int32, (tile, LANES), 1)
    puts = []
    for step in range(mine.shape[0] // tile)[::-1]:
        here = slice(step * tile, (step + 1) * tile)
        blocks = min(n_row, ((4 * step + 3) * n_row + n_row - 1) // n_col + 1)
        blocks = -(-blocks * LANES // WIDE) * (WIDE // LANES)
        for half, other_half in ((mine, 0), (other, 1)):
            q = 4 * step + 2 * (parity if other_half == 0 else 1 - parity)
            first_row = (q * n_row + row_at) * stretch
            slot = len(puts)
            row_norm[...] = row_norms(half[here, width:], scale)
            for at in range(0, blocks * LANES, WIDE):
                to = slice(at, at + WIDE)
                update = nt_dot(half[here, :width], factor_ref[to, :])
                inner = nt_dot(half[here, width:], col_ref[to, :])
                result = gauss(scale, inner, row_norm[...], norms[:1, to]) - update
                for b in range(WIDE // LANES):
                    block = at // LANES + b
                    first_col = (block * n_col + col_at) * stretch
                    piece = result[:, b * LANES : (b + 1) * LANES]
                    piece = jnp.where(above >= first_col - first_row, piece, 0.0)
                    stage[slot, pl.ds(block, tile, stride=n_row), :] = piece
            for block in range(blocks, n_row):
                stage[slot, pl.ds(block, tile, stride=n_row), :] = jnp.zeros((tile, LANES), F32)
            to = pl.ds(pl.multiple_of(q * (stretch * n_row), stretch * n_row), tile * n_row)
            puts.append(pltpu.make_async_copy(stage.at[slot], out_hbm.at[to], out_sems.at[slot]))
            puts[-1].start()
    for put in puts:
        put.wait()


def shards(teacher, panel_ids, rest_ids, inverse):
    n_row, n_col = lax.axis_size("row"), lax.axis_size("col")
    stretch = rest_ids.shape[2]
    width = inverse.shape[0]
    emb = teacher.shape[1]
    n_rows, n_cols = n_col * stretch, n_row * stretch
    half = n_rows // 2
    scale = 2.0 / emb * math.log2(math.e)
    vmem = pl.BlockSpec(memory_space=pltpu.VMEM)
    hbm = pl.BlockSpec(memory_space=pl.ANY)
    near = functools.partial(pltpu.with_memory_space_constraint, memory_space=pltpu.VMEM)
    far = functools.partial(pltpu.with_memory_space_constraint, memory_space=pltpu.HBM)
    both = jnp.concatenate([rest_ids.reshape(1, 1, -1), panel_ids.reshape(1, 1, -1)], 0)
    both = jnp.broadcast_to(both[None], (n_row * n_col, *both.shape))
    both = lax.all_to_all(both, ("row", "col"), 0, 0, tiled=True)

    mine, panel_emb, panel_norms, col_emb, inverse_near = pl.pallas_call(
        functools.partial(rows_kernel, scale, (n_col, n_col, n_row)),
        out_shape=(
            pltpu.VMEM((half, width + emb), BF16),
            pltpu.VMEM((width, emb), BF16),
            pltpu.VMEM((8, width), F32),
            pltpu.VMEM((n_cols, emb), BF16),
            pltpu.VMEM((width, width), BF16),
        ),
        in_specs=[hbm] * 5,
        out_specs=[vmem] * 5,
        scratch_shapes=[
            pltpu.VMEM((teacher.shape[0] // PIECE, PIECE, emb), BF16),
            pltpu.VMEM((teacher.shape[0], LANES), F32),
            pltpu.VMEM((teacher.shape[0], LANES), F32),
            pltpu.VMEM((2, stretch, LANES), F32),
            pltpu.VMEM((2, stretch, LANES), F32),
            pltpu.VMEM((half, LANES), F32),
            pltpu.VMEM((half, width), BF16),
            pltpu.SMEM((2 * n_col + n_row, 1, stretch), jnp.int32),
            pltpu.SemaphoreType.DMA((3,)),
            pltpu.SemaphoreType.DMA((teacher.shape[0] // PIECE,)),
            pltpu.SemaphoreType.DMA((width // WIDE,)),
        ],
        compiler_params=pltpu.CompilerParams(vmem_limit_bytes=38 * MIB),
        name="rows",
    )(far(teacher), far(inverse), both, both.reshape(n_col, n_row, 2, 1, stretch),
      both.reshape(n_row, n_col, 2, 1, stretch))

    other = lax.ppermute(mine, "col", [(i, i ^ 1) for i in range(n_col)])

    factors, own = pl.pallas_call(
        functools.partial(column_kernel, scale, stretch),
        out_shape=(
            pltpu.VMEM((n_cols, width), BF16),
            jax.ShapeDtypeStruct((stretch, width), BF16),
        ),
        in_specs=[vmem] * 4,
        out_specs=[vmem, hbm],
        scratch_shapes=[
            pltpu.VMEM((n_cols, LANES), F32),
            pltpu.VMEM((n_cols, width), BF16),
            pltpu.SemaphoreType.DMA((width // WIDE,)),
        ],
        compiler_params=pltpu.CompilerParams(vmem_limit_bytes=14 * MIB),
        cost_estimate=pl.CostEstimate(
            flops=2 * n_cols * width * width, bytes_accessed=16 * MIB, transcendentals=n_cols * width),
        name="columns",
    )(near(col_emb), near(panel_emb), near(panel_norms), near(inverse_near))

    trailing = pl.pallas_call(
        functools.partial(update_kernel, scale, n_row, n_col, stretch),
        out_shape=jax.ShapeDtypeStruct((n_rows * n_row, stretch), F32),
        in_specs=[vmem] * 4,
        out_specs=hbm,
        scratch_shapes=[
            pltpu.VMEM((n_col // 2, 2 * stretch * n_row, stretch), F32),
            pltpu.VMEM((8, n_cols), F32),
            pltpu.VMEM((2 * stretch, LANES), F32),
            pltpu.SemaphoreType.DMA((n_col // 2,)),
        ],
        compiler_params=pltpu.CompilerParams(vmem_limit_bytes=20 * MIB),
        name="update",
    )(near(mine), near(other), near(factors), near(col_emb))
    return (
        trailing.reshape(n_col, 1, stretch, n_row, 1, stretch),
        own.reshape(1, 1, stretch, width),
    )


def solution(mesh):
    return jax.shard_map(
        shards,
        mesh=mesh,
        in_specs=(P(), P("col"), P("row", "col", None), P()),
        out_specs=(P(None, "row", None, None, "col", None), P("row", "col", None, None)),
        check_vma=False,
    )
```

```python
import functools
import math

import jax
import jax.numpy as jnp
from jax import lax
from jax.experimental import pallas as pl
from jax.experimental.pallas import tpu as pltpu
from jax.sharding import PartitionSpec as P

BF16, F32 = jnp.bfloat16, jnp.float32
MIB = 1 << 20
LANES = 128
WIDE = 256
PIECE = 1024


def nt_dot(left, right):
    return lax.dot_general(left, right, (((1,), (1,)), ((), ())), preferred_element_type=F32)


def split_squares(rows):
    wide = rows.astype(F32)
    square = wide * wide
    high = square.astype(BF16)
    return high, (square - high.astype(F32)).astype(BF16)


def row_norms(rows, scale):
    high, low = split_squares(rows)
    ones = jnp.ones((LANES, rows.shape[1]), BF16)
    return scale * (nt_dot(high, ones) + nt_dot(low, ones))


def lane_norms(rows, scale):
    high, low = split_squares(rows)
    ones = jnp.ones((8, rows.shape[1]), BF16)
    return scale * (nt_dot(ones, high) + nt_dot(ones, low))


def gauss(scale, inner, norms, other_norms):
    norms = jnp.concatenate([norms] * (inner.shape[1] // LANES), 1)
    return jnp.exp2(2.0 * scale * inner - norms - other_norms)


def start_load(teacher, inverse, inverse_out, pieces, sems, inverse_sems):
    copies = [
        pltpu.make_async_copy(teacher.at[pl.ds(i * PIECE, PIECE)], pieces.at[i], sems.at[i])
        for i in range(pieces.shape[0])
    ]
    inverse_copies = []
    for i in range(inverse.shape[0] // WIDE):
        at = (pl.ds(i * WIDE, WIDE), pl.ds(0, (i + 1) * WIDE))
        inverse_copies.append(pltpu.make_async_copy(inverse.at[at], inverse_out.at[at], inverse_sems.at[i]))
    for copy in copies:
        copy.start()
    return copies, inverse_copies


def widen(copies, pieces, left, right):
    for i, copy in enumerate(copies):
        copy.wait()

        def step(part, carry):
            at = pl.ds(pl.multiple_of(part * WIDE, WIDE), WIDE)
            to = pl.ds(pl.multiple_of(i * PIECE + part * WIDE, WIDE), WIDE)
            left[to, :] = pieces[i, at, :LANES].astype(F32)
            right[to, :] = pieces[i, at, LANES:].astype(F32)
            return carry

        lax.fori_loop(0, PIECE // WIDE, step, 0)


def gather_blocks(ids, tables, stages, id_block, count, out, column):
    stretch, slots = ids.shape[2], stages[0].shape[0]

    def one(i, carry):
        for b in range(slots):
            block = id_block(i, b)
            for u in range(stretch):
                row = ids[block, 0, u]
                for table, stage in zip(tables, stages):
                    stage[b, u : u + 1, :] = table[pl.ds(row, 1), :]
            to = pl.ds(pl.multiple_of((slots * i + b) * stretch, stretch), stretch)
            for k, stage in enumerate(stages):
                out[to, column + k * LANES : column + (k + 1) * LANES] = stage[b].astype(BF16)
        return carry

    lax.fori_loop(0, count // slots, one, 0)


def rows_kernel(scale, n_sets, teacher, inverse, panel_ids, row_ids, col_ids,
                half_out, panel_out, norm_out, col_out, inverse_ref, norms,
                pieces, left, right, stage_left, stage_right, cross, ids, sems, piece_sems, inverse_sems):
    row_at, col_at = lax.axis_index("row"), lax.axis_index("col")
    n_panel, n_rows, n_cols = n_sets
    copies = [
        pltpu.make_async_copy(panel_ids.at[pl.ds(0, n_panel), 1], ids.at[pl.ds(0, n_panel)], sems.at[0]),
        pltpu.make_async_copy(row_ids.at[:, row_at, 0], ids.at[pl.ds(n_panel, n_rows)], sems.at[1]),
        pltpu.make_async_copy(col_ids.at[:, col_at, 0], ids.at[pl.ds(n_panel + n_rows, n_cols)], sems.at[2]),
    ]
    for copy in copies:
        copy.start()
    piece_copies, inverse_copies = start_load(teacher, inverse, inverse_ref, pieces, piece_sems, inverse_sems)
    widen(piece_copies, pieces, left, right)
    for copy in inverse_copies:
        copy.start()
    for copy in copies:
        copy.wait()
    width = panel_out.shape[0]

    take = functools.partial(gather_blocks, ids, (left, right), (stage_left, stage_right))
    slots = stage_left.shape[0]
    take(lambda i, b: n_panel + 2 * slots * i + 4 * (b // 2) + b % 2 + 2 * (col_at % 2), n_rows // 2, half_out, width)
    take(lambda i, b: slots * i + b, n_panel, panel_out, 0)
    take(lambda i, b: n_panel + n_rows + slots * i + b, n_cols, col_out, 0)
    norms[...] = row_norms(half_out[:, width:], scale)
    for at in range(0, width, WIDE):
        norm_out[:, at : at + WIDE] = lane_norms(panel_out[at : at + WIDE, :], scale)
    for copy in inverse_copies:
        copy.wait()
    cross_rows(scale, lambda: half_out[:, width:], norms, panel_out, norm_out, cross)
    for j in range(width // WIDE):
        factor_columns(j, inverse_ref, cross, half_out)


def cross_rows(scale, rows, norms, panel_ref, norm_ref, cross):
    for at in range(0, panel_ref.shape[0], WIDE):
        to = slice(at, at + WIDE)
        cross[:, to] = gauss(scale, nt_dot(rows(), panel_ref[to, :]), norms[...], norm_ref[:1, to]).astype(BF16)


def factor_columns(j, inverse_ref, cross, factor_ref):
    to, depth = slice(j * WIDE, (j + 1) * WIDE), (j + 1) * WIDE
    factor_ref[:, to] = nt_dot(cross[:, :depth], inverse_ref[to, :depth]).astype(BF16)


def column_kernel(scale, n_row, n_col, stretch, col_ref, panel_ref, norm_ref, inverse_ref, mine, mine_norms,
                  factor_out, col_norms, first_out, norms, cross):
    norms[...] = row_norms(col_ref[...], scale)
    for at in range(0, col_ref.shape[0], WIDE):
        col_norms[:, at : at + WIDE] = lane_norms(col_ref[at : at + WIDE, :], scale)
    cross_rows(scale, lambda: col_ref[...], norms, panel_ref, norm_ref, cross)
    for j in range(panel_ref.shape[0] // WIDE):
        factor_columns(j, inverse_ref, cross, factor_out)
    step = mine.shape[0] // (2 * stretch) - 1
    update_tile(scale, n_row, n_col, stretch, step, lax.axis_index("col") % 2, mine, mine_norms,
                factor_out, col_ref, col_norms, first_out)


def update_tile(scale, n_row, n_col, stretch, step, pair, half, row_norm, factor_ref, col_ref, norms, stage):
    row_at, col_at = lax.axis_index("row"), lax.axis_index("col")
    width, tile = factor_ref.shape[1], 2 * stretch
    here = slice(step * tile, (step + 1) * tile)
    first_row = ((4 * step + 2 * pair) * n_row + row_at) * stretch
    above = lax.broadcasted_iota(jnp.int32, (tile, LANES), 0)
    above = above // stretch * (n_row * stretch) + above % stretch - lax.broadcasted_iota(jnp.int32, (tile, LANES), 1)
    blocks = min(n_row, ((4 * step + 3) * n_row + n_row - 1) // n_col + 1)
    blocks = -(-blocks * LANES // WIDE) * (WIDE // LANES)
    for at in range(0, blocks * LANES, WIDE):
        to = slice(at, at + WIDE)
        update = nt_dot(half[here, :width], factor_ref[to, :])
        inner = nt_dot(half[here, width:], col_ref[to, :])
        result = gauss(scale, inner, row_norm[here, :], norms[:1, to]) - update
        for b in range(WIDE // LANES):
            block = at // LANES + b
            first_col = (block * n_col + col_at) * stretch
            piece = result[:, b * LANES : (b + 1) * LANES]
            piece = jnp.where(above >= first_col - first_row, piece, 0.0)
            stage[pl.ds(block, tile, stride=n_row), :] = piece
    for block in range(blocks, n_row):
        stage[pl.ds(block, tile, stride=n_row), :] = jnp.zeros((tile, LANES), F32)


def update_kernel(scale, n_row, n_col, stretch, mine, other, factor_ref, col_ref, mine_norms, norms, first,
                  out_hbm, own_out, stage, other_norms, out_sems, own_sem):
    parity = lax.axis_index("col") % 2
    width = factor_ref.shape[1]
    size = first.shape[0]
    own = pl.ds(pl.multiple_of(lax.axis_index("row") * stretch, stretch), stretch)
    puts = []

    def put(step, pair, ref):
        at = (4 * step + 2 * pair) * (stretch * n_row)
        to = pl.ds(pl.multiple_of(at, stretch * n_row), size)
        puts.append(pltpu.make_async_copy(ref, out_hbm.at[to], out_sems.at[len(puts)]))
        puts[-1].start()

    steps = mine.shape[0] // (2 * stretch)
    put(steps - 1, parity, first)
    own_copy = pltpu.make_async_copy(factor_ref.at[own], own_out, own_sem)
    own_copy.start()
    other_norms[...] = row_norms(other[:, width:], scale)
    for step in range(steps)[::-1]:
        for pair, half, row_norm in ((parity, mine, mine_norms), (1 - parity, other, other_norms)):
            if step == steps - 1 and half is mine:
                continue
            slot = stage.at[len(puts) - 1]
            update_tile(scale, n_row, n_col, stretch, step, pair, half, row_norm, factor_ref, col_ref, norms, slot)
            put(step, pair, slot)
    own_copy.wait()
    for copy in puts:
        copy.wait()


def shards(teacher, panel_ids, rest_ids, inverse):
    n_row, n_col = lax.axis_size("row"), lax.axis_size("col")
    stretch = rest_ids.shape[2]
    width = inverse.shape[0]
    emb = teacher.shape[1]
    n_rows, n_cols = n_col * stretch, n_row * stretch
    half = n_rows // 2
    scale = 2.0 / emb * math.log2(math.e)
    vmem = pl.BlockSpec(memory_space=pltpu.VMEM)
    hbm = pl.BlockSpec(memory_space=pl.ANY)
    near = functools.partial(pltpu.with_memory_space_constraint, memory_space=pltpu.VMEM)
    far = functools.partial(pltpu.with_memory_space_constraint, memory_space=pltpu.HBM)
    wide = (n_row * n_col, 2, 1, stretch)
    which = lax.broadcasted_iota(jnp.int32, wide, 1)
    both = jnp.where(which == 0, rest_ids.reshape(1, 1, 1, -1), panel_ids.reshape(1, 1, 1, -1))
    both = lax.all_to_all(both, ("row", "col"), 0, 0, tiled=True)

    n_table = teacher.shape[0]
    mine, panel_emb, panel_norms, col_emb, inverse_near, mine_norms = pl.pallas_call(
        functools.partial(rows_kernel, scale, (n_col, n_col, n_row)),
        out_shape=(
            pltpu.VMEM((half, width + emb), BF16),
            pltpu.VMEM((width, emb), BF16),
            pltpu.VMEM((8, width), F32),
            pltpu.VMEM((n_cols, emb), BF16),
            pltpu.VMEM((width, width), BF16),
            pltpu.VMEM((half, LANES), F32),
        ),
        in_specs=[hbm] * 5,
        out_specs=[vmem] * 6,
        scratch_shapes=[
            pltpu.VMEM((n_table // PIECE, PIECE, emb), BF16),
            pltpu.VMEM((n_table, LANES), F32),
            pltpu.VMEM((n_table, LANES), F32),
            pltpu.VMEM((4, stretch, LANES), F32),
            pltpu.VMEM((4, stretch, LANES), F32),
            pltpu.VMEM((half, width), BF16),
            pltpu.SMEM((2 * n_col + n_row, 1, stretch), jnp.int32),
            pltpu.SemaphoreType.DMA((3,)),
            pltpu.SemaphoreType.DMA((n_table // PIECE,)),
            pltpu.SemaphoreType.DMA((width // WIDE,)),
        ],
        compiler_params=pltpu.CompilerParams(vmem_limit_bytes=36 * MIB),
        name="rows",
    )(far(teacher), far(inverse), both, both.reshape(n_col, n_row, 2, 1, stretch),
      both.reshape(n_row, n_col, 2, 1, stretch))

    other = lax.ppermute(mine, "col", [(i, i ^ 1) for i in range(n_col)])

    size = 2 * stretch * n_row
    factors, col_norms, first = pl.pallas_call(
        functools.partial(column_kernel, scale, n_row, n_col, stretch),
        out_shape=(
            pltpu.VMEM((n_cols, width), BF16),
            pltpu.VMEM((8, n_cols), F32),
            pltpu.VMEM((size, stretch), F32),
        ),
        in_specs=[vmem] * 6,
        out_specs=[vmem] * 3,
        scratch_shapes=[
            pltpu.VMEM((n_cols, LANES), F32),
            pltpu.VMEM((n_cols, width), BF16),
        ],
        compiler_params=pltpu.CompilerParams(vmem_limit_bytes=14 * MIB),
        cost_estimate=pl.CostEstimate(
            flops=2 * n_cols * width * width, bytes_accessed=16 * MIB, transcendentals=n_cols * width),
        name="columns",
    )(near(col_emb), near(panel_emb), near(panel_norms), near(inverse_near), near(mine), near(mine_norms))

    trailing, own = pl.pallas_call(
        functools.partial(update_kernel, scale, n_row, n_col, stretch),
        out_shape=(
            jax.ShapeDtypeStruct((n_rows * n_row, stretch), F32),
            jax.ShapeDtypeStruct((stretch, width), BF16),
        ),
        in_specs=[vmem] * 7,
        out_specs=[hbm] * 2,
        scratch_shapes=[
            pltpu.VMEM((n_col // 2 - 1, size, stretch), F32),
            pltpu.VMEM((half, LANES), F32),
            pltpu.SemaphoreType.DMA((n_col // 2,)),
            pltpu.SemaphoreType.DMA,
        ],
        compiler_params=pltpu.CompilerParams(vmem_limit_bytes=20 * MIB),
        name="update",
    )(near(mine), near(other), near(factors), near(col_emb), near(mine_norms), near(col_norms), near(first))
    return (
        trailing.reshape(n_col, 1, stretch, n_row, 1, stretch),
        own.reshape(1, 1, stretch, width),
    )


def solution(mesh):
    return jax.shard_map(
        shards,
        mesh=mesh,
        in_specs=(P(), P("col"), P("row", "col", None), P()),
        out_specs=(P(None, "row", None, None, "col", None), P("row", "col", None, None)),
        check_vma=False,
    )
```

```python
import functools
import math

import jax
import jax.numpy as jnp
from jax import lax
from jax.experimental import pallas as pl
from jax.experimental.pallas import tpu as pltpu
from jax.sharding import PartitionSpec as P

BF16, F32 = jnp.bfloat16, jnp.float32
MIB = 1 << 20
LANES = 128
WIDE = 256
PIECE = 1024


def nt_dot(left, right):
    return lax.dot_general(left, right, (((1,), (1,)), ((), ())), preferred_element_type=F32)


def split_squares(rows):
    wide = rows.astype(F32)
    square = wide * wide
    high = square.astype(BF16)
    return high, (square - high.astype(F32)).astype(BF16)


def row_norms(rows, scale):
    high, low = split_squares(rows)
    ones = jnp.ones((LANES, rows.shape[1]), BF16)
    return scale * (nt_dot(high, ones) + nt_dot(low, ones))


def lane_norms(rows, scale):
    high, low = split_squares(rows)
    ones = jnp.ones((8, rows.shape[1]), BF16)
    return scale * (nt_dot(ones, high) + nt_dot(ones, low))


def gauss(scale, inner, norms, other_norms):
    norms = jnp.concatenate([norms] * (inner.shape[1] // LANES), 1)
    return jnp.exp2(2.0 * scale * inner - norms - other_norms)


def start_load(teacher, inverse, inverse_out, pieces, sems, inverse_sems):
    copies = [
        pltpu.make_async_copy(teacher.at[pl.ds(i * PIECE, PIECE)], pieces.at[i], sems.at[i])
        for i in range(pieces.shape[0])
    ]
    inverse_copies = []
    for i in range(inverse.shape[0] // WIDE):
        at = (pl.ds(i * WIDE, WIDE), pl.ds(0, (i + 1) * WIDE))
        inverse_copies.append(pltpu.make_async_copy(inverse.at[at], inverse_out.at[at], inverse_sems.at[i]))
    for copy in copies:
        copy.start()
    return copies, inverse_copies


def widen(copies, pieces, left, right):
    for i, copy in enumerate(copies):
        copy.wait()

        def step(part, carry):
            at = pl.ds(pl.multiple_of(part * WIDE, WIDE), WIDE)
            to = pl.ds(pl.multiple_of(i * PIECE + part * WIDE, WIDE), WIDE)
            left[to, :] = pieces[i, at, :LANES].astype(F32)
            right[to, :] = pieces[i, at, LANES:].astype(F32)
            return carry

        lax.fori_loop(0, PIECE // WIDE, step, 0)


def gather_blocks(ids, tables, stages, id_block, count, out, column):
    stretch, slots = ids.shape[2], stages[0].shape[0]

    def one(i, carry):
        for b in range(slots):
            block = id_block(i, b)
            for u in range(stretch):
                row = ids[block, 0, u]
                for table, stage in zip(tables, stages):
                    stage[b, u : u + 1, :] = table[pl.ds(row, 1), :]
            to = pl.ds(pl.multiple_of((slots * i + b) * stretch, stretch), stretch)
            for k, stage in enumerate(stages):
                out[to, column + k * LANES : column + (k + 1) * LANES] = stage[b].astype(BF16)
        return carry

    lax.fori_loop(0, count // slots, one, 0)


def rows_kernel(scale, n_sets, teacher, inverse, panel_ids, row_ids, col_ids,
                half_out, panel_out, norm_out, col_out, inverse_ref, norms,
                pieces, left, right, stage_left, stage_right, cross, ids, sems, piece_sems, inverse_sems):
    row_at, col_at = lax.axis_index("row"), lax.axis_index("col")
    n_panel, n_rows, n_cols = n_sets
    copies = [
        pltpu.make_async_copy(panel_ids.at[pl.ds(0, n_panel), 1], ids.at[pl.ds(0, n_panel)], sems.at[0]),
        pltpu.make_async_copy(row_ids.at[:, row_at, 0], ids.at[pl.ds(n_panel, n_rows)], sems.at[1]),
        pltpu.make_async_copy(col_ids.at[:, col_at, 0], ids.at[pl.ds(n_panel + n_rows, n_cols)], sems.at[2]),
    ]
    for copy in copies:
        copy.start()
    piece_copies, inverse_copies = start_load(teacher, inverse, inverse_ref, pieces, piece_sems, inverse_sems)
    widen(piece_copies, pieces, left, right)
    for copy in inverse_copies:
        copy.start()
    for copy in copies:
        copy.wait()
    width = panel_out.shape[0]

    take = functools.partial(gather_blocks, ids, (left, right), (stage_left, stage_right))
    slots = stage_left.shape[0]
    take(lambda i, b: n_panel + 2 * slots * i + 4 * (b // 2) + b % 2 + 2 * (col_at % 2), n_rows // 2, half_out, width)
    take(lambda i, b: slots * i + b, n_panel, panel_out, 0)
    take(lambda i, b: n_panel + n_rows + slots * i + b, n_cols, col_out, 0)
    norms[...] = row_norms(half_out[:, width:], scale)
    for at in range(0, width, WIDE):
        norm_out[:, at : at + WIDE] = lane_norms(panel_out[at : at + WIDE, :], scale)
    for copy in inverse_copies:
        copy.wait()
    cross_rows(scale, lambda: half_out[:, width:], norms, panel_out, norm_out, cross)
    for j in range(width // WIDE):
        factor_columns(j, inverse_ref, cross, half_out)


def cross_rows(scale, rows, norms, panel_ref, norm_ref, cross):
    for at in range(0, panel_ref.shape[0], WIDE):
        to = slice(at, at + WIDE)
        cross[:, to] = gauss(scale, nt_dot(rows(), panel_ref[to, :]), norms[...], norm_ref[:1, to]).astype(BF16)


def factor_columns(j, inverse_ref, cross, factor_ref):
    to, depth = slice(j * WIDE, (j + 1) * WIDE), (j + 1) * WIDE
    factor_ref[:, to] = nt_dot(cross[:, :depth], inverse_ref[to, :depth]).astype(BF16)


def column_kernel(scale, n_row, n_col, stretch, col_ref, panel_ref, norm_ref, inverse_ref, mine, mine_norms,
                  factor_out, col_norms, first_out, norms, cross):
    norms[...] = row_norms(col_ref[...], scale)
    for at in range(0, col_ref.shape[0], WIDE):
        col_norms[:, at : at + WIDE] = lane_norms(col_ref[at : at + WIDE, :], scale)
    cross_rows(scale, lambda: col_ref[...], norms, panel_ref, norm_ref, cross)
    for j in range(panel_ref.shape[0] // WIDE):
        factor_columns(j, inverse_ref, cross, factor_out)
    step = mine.shape[0] // (2 * stretch) - 1
    update_tile(scale, n_row, n_col, stretch, step, lax.axis_index("col") % 2, mine, mine_norms,
                factor_out, col_ref, col_norms, first_out)


def update_tile(scale, n_row, n_col, stretch, step, pair, half, row_norm, factor_ref, col_ref, norms, stage):
    row_at, col_at = lax.axis_index("row"), lax.axis_index("col")
    width, tile = factor_ref.shape[1], 2 * stretch
    here = slice(step * tile, (step + 1) * tile)
    first_row = ((4 * step + 2 * pair) * n_row + row_at) * stretch
    above = lax.broadcasted_iota(jnp.int32, (tile, LANES), 0)
    above = above // stretch * (n_row * stretch) + above % stretch - lax.broadcasted_iota(jnp.int32, (tile, LANES), 1)
    blocks = min(n_row, ((4 * step + 3) * n_row + n_row - 1) // n_col + 1)
    blocks = -(-blocks * LANES // WIDE) * (WIDE // LANES)
    for at in range(0, blocks * LANES, WIDE):
        to = slice(at, at + WIDE)
        update = nt_dot(half[here, :width], factor_ref[to, :])
        inner = nt_dot(half[here, width:], col_ref[to, :])
        result = gauss(scale, inner, row_norm[here, :], norms[:1, to]) - update
        for b in range(WIDE // LANES):
            block = at // LANES + b
            first_col = (block * n_col + col_at) * stretch
            piece = result[:, b * LANES : (b + 1) * LANES]
            piece = jnp.where(above >= first_col - first_row, piece, 0.0)
            stage[pl.ds(block, tile, stride=n_row), :] = piece
    for block in range(blocks, n_row):
        stage[pl.ds(block, tile, stride=n_row), :] = jnp.zeros((tile, LANES), F32)


def update_kernel(scale, n_row, n_col, stretch, mine, other, factor_ref, col_ref, mine_norms, norms, first,
                  out_hbm, own_out, stage, other_norms, out_sems, own_sem):
    parity = lax.axis_index("col") % 2
    width = factor_ref.shape[1]
    size = first.shape[0]
    own = pl.ds(pl.multiple_of(lax.axis_index("row") * stretch, stretch), stretch)
    puts = []

    def put(step, pair, ref):
        at = (4 * step + 2 * pair) * (stretch * n_row)
        to = pl.ds(pl.multiple_of(at, stretch * n_row), size)
        puts.append(pltpu.make_async_copy(ref, out_hbm.at[to], out_sems.at[len(puts)]))
        puts[-1].start()

    steps = mine.shape[0] // (2 * stretch)
    put(steps - 1, parity, first)
    own_copy = pltpu.make_async_copy(factor_ref.at[own], own_out, own_sem)
    own_copy.start()
    other_norms[...] = row_norms(other[:, width:], scale)
    for step in range(steps)[::-1]:
        for pair, half, row_norm in ((parity, mine, mine_norms), (1 - parity, other, other_norms)):
            if step == steps - 1 and half is mine:
                continue
            slot = stage.at[len(puts) - 1]
            update_tile(scale, n_row, n_col, stretch, step, pair, half, row_norm, factor_ref, col_ref, norms, slot)
            put(step, pair, slot)
    own_copy.wait()
    for copy in puts:
        copy.wait()


def shards(teacher, panel_ids, rest_ids, inverse):
    n_row, n_col = lax.axis_size("row"), lax.axis_size("col")
    stretch = rest_ids.shape[2]
    width = inverse.shape[0]
    emb = teacher.shape[1]
    n_rows, n_cols = n_col * stretch, n_row * stretch
    half = n_rows // 2
    scale = 2.0 / emb * math.log2(math.e)
    vmem = pl.BlockSpec(memory_space=pltpu.VMEM)
    hbm = pl.BlockSpec(memory_space=pl.ANY)
    near = functools.partial(pltpu.with_memory_space_constraint, memory_space=pltpu.VMEM)
    far = functools.partial(pltpu.with_memory_space_constraint, memory_space=pltpu.HBM)
    wide = (n_row * n_col, 2, 1, stretch)
    which = lax.iota(jnp.int32, math.prod(wide)).reshape(wide) // stretch % 2
    both = jnp.where(which == 0, rest_ids.reshape(1, 1, 1, -1), panel_ids.reshape(1, 1, 1, -1))
    both = lax.all_to_all(both, ("row", "col"), 0, 0, tiled=True)

    n_table = teacher.shape[0]
    mine, panel_emb, panel_norms, col_emb, inverse_near, mine_norms = pl.pallas_call(
        functools.partial(rows_kernel, scale, (n_col, n_col, n_row)),
        out_shape=(
            pltpu.VMEM((half, width + emb), BF16),
            pltpu.VMEM((width, emb), BF16),
            pltpu.VMEM((8, width), F32),
            pltpu.VMEM((n_cols, emb), BF16),
            pltpu.VMEM((width, width), BF16),
            pltpu.VMEM((half, LANES), F32),
        ),
        in_specs=[hbm] * 5,
        out_specs=[vmem] * 6,
        scratch_shapes=[
            pltpu.VMEM((n_table // PIECE, PIECE, emb), BF16),
            pltpu.VMEM((n_table, LANES), F32),
            pltpu.VMEM((n_table, LANES), F32),
            pltpu.VMEM((8, stretch, LANES), F32),
            pltpu.VMEM((8, stretch, LANES), F32),
            pltpu.VMEM((half, width), BF16),
            pltpu.SMEM((2 * n_col + n_row, 1, stretch), jnp.int32),
            pltpu.SemaphoreType.DMA((3,)),
            pltpu.SemaphoreType.DMA((n_table // PIECE,)),
            pltpu.SemaphoreType.DMA((width // WIDE,)),
        ],
        compiler_params=pltpu.CompilerParams(vmem_limit_bytes=36 * MIB),
        name="rows",
    )(far(teacher), far(inverse), both, both.reshape(n_col, n_row, 2, 1, stretch),
      both.reshape(n_row, n_col, 2, 1, stretch))

    other = lax.ppermute(mine, "col", [(i, i ^ 1) for i in range(n_col)])

    size = 2 * stretch * n_row
    factors, col_norms, first = pl.pallas_call(
        functools.partial(column_kernel, scale, n_row, n_col, stretch),
        out_shape=(
            pltpu.VMEM((n_cols, width), BF16),
            pltpu.VMEM((8, n_cols), F32),
            pltpu.VMEM((size, stretch), F32),
        ),
        in_specs=[vmem] * 6,
        out_specs=[vmem] * 3,
        scratch_shapes=[
            pltpu.VMEM((n_cols, LANES), F32),
            pltpu.VMEM((n_cols, width), BF16),
        ],
        compiler_params=pltpu.CompilerParams(vmem_limit_bytes=14 * MIB),
        cost_estimate=pl.CostEstimate(
            flops=2 * n_cols * width * width, bytes_accessed=16 * MIB, transcendentals=n_cols * width),
        name="columns",
    )(near(col_emb), near(panel_emb), near(panel_norms), near(inverse_near), near(mine), near(mine_norms))

    trailing, own = pl.pallas_call(
        functools.partial(update_kernel, scale, n_row, n_col, stretch),
        out_shape=(
            jax.ShapeDtypeStruct((n_rows * n_row, stretch), F32),
            jax.ShapeDtypeStruct((stretch, width), BF16),
        ),
        in_specs=[vmem] * 7,
        out_specs=[hbm] * 2,
        scratch_shapes=[
            pltpu.VMEM((n_col // 2 - 1, size, stretch), F32),
            pltpu.VMEM((half, LANES), F32),
            pltpu.SemaphoreType.DMA((n_col // 2,)),
            pltpu.SemaphoreType.DMA,
        ],
        compiler_params=pltpu.CompilerParams(vmem_limit_bytes=20 * MIB),
        name="update",
    )(near(mine), near(other), near(factors), near(col_emb), near(mine_norms), near(col_norms), near(first))
    return (
        trailing.reshape(n_col, 1, stretch, n_row, 1, stretch),
        own.reshape(1, 1, stretch, width),
    )


def solution(mesh):
    return jax.shard_map(
        shards,
        mesh=mesh,
        in_specs=(P(), P("col"), P("row", "col", None), P()),
        out_specs=(P(None, "row", None, None, "col", None), P("row", "col", None, None)),
        check_vma=False,
    )
```

```python
import functools
import math

import jax
import jax.numpy as jnp
from jax import lax
from jax.experimental import pallas as pl
from jax.experimental.pallas import tpu as pltpu
from jax.sharding import PartitionSpec as P

BF16, F32 = jnp.bfloat16, jnp.float32
MIB = 1 << 20
LANES = 128
WIDE = 256
PIECE = 1024


def nt_dot(left, right):
    return lax.dot_general(left, right, (((1,), (1,)), ((), ())), preferred_element_type=F32)


def split_squares(rows):
    wide = rows.astype(F32)
    square = wide * wide
    high = square.astype(BF16)
    return high, (square - high.astype(F32)).astype(BF16)


def row_norms(rows, scale):
    high, low = split_squares(rows)
    ones = jnp.ones((LANES, rows.shape[1]), BF16)
    return scale * (nt_dot(high, ones) + nt_dot(low, ones))


def lane_norms(rows, scale):
    high, low = split_squares(rows)
    ones = jnp.ones((8, rows.shape[1]), BF16)
    return scale * (nt_dot(ones, high) + nt_dot(ones, low))


def gauss(scale, inner, norms, other_norms):
    norms = jnp.concatenate([norms] * (inner.shape[1] // LANES), 1)
    return jnp.exp2(2.0 * scale * inner - norms - other_norms)


def start_load(teacher, inverse, inverse_out, pieces, sems, inverse_sems):
    copies = [
        pltpu.make_async_copy(teacher.at[pl.ds(i * PIECE, PIECE)], pieces.at[i], sems.at[i])
        for i in range(pieces.shape[0])
    ]
    inverse_copies = []
    for i in range(inverse.shape[0] // WIDE):
        at = (pl.ds(i * WIDE, WIDE), pl.ds(0, (i + 1) * WIDE))
        inverse_copies.append(pltpu.make_async_copy(inverse.at[at], inverse_out.at[at], inverse_sems.at[i]))
    for copy in copies:
        copy.start()
    return copies, inverse_copies


def widen(copies, pieces, left, right):
    for i, copy in enumerate(copies):
        copy.wait()

        def step(part, carry):
            at = pl.ds(pl.multiple_of(part * WIDE, WIDE), WIDE)
            to = pl.ds(pl.multiple_of(i * PIECE + part * WIDE, WIDE), WIDE)
            left[to, :] = pieces[i, at, :LANES].astype(F32)
            right[to, :] = pieces[i, at, LANES:].astype(F32)
            return carry

        lax.fori_loop(0, PIECE // WIDE, step, 0)


def gather_blocks(ids, tables, stages, id_block, count, out, column):
    stretch, slots = ids.shape[2], stages[0].shape[0]

    def one(i, carry):
        for b in range(slots):
            block = id_block(i, b)
            for u in range(stretch):
                row = ids[block, 0, u]
                for table, stage in zip(tables, stages):
                    stage[b, u : u + 1, :] = table[pl.ds(row, 1), :]
            to = pl.ds(pl.multiple_of((slots * i + b) * stretch, stretch), stretch)
            for k, stage in enumerate(stages):
                out[to, column + k * LANES : column + (k + 1) * LANES] = stage[b].astype(BF16)
        return carry

    lax.fori_loop(0, count // slots, one, 0)


def rows_kernel(scale, n_sets, teacher, inverse, panel_ids, row_ids, col_ids,
                half_out, panel_out, norm_out, col_out, inverse_ref, norms,
                pieces, left, right, stage_left, stage_right, cross, ids, sems, piece_sems, inverse_sems):
    row_at, col_at = lax.axis_index("row"), lax.axis_index("col")
    n_panel, n_rows, n_cols = n_sets
    copies = [
        pltpu.make_async_copy(panel_ids.at[pl.ds(0, n_panel), 1], ids.at[pl.ds(0, n_panel)], sems.at[0]),
        pltpu.make_async_copy(row_ids.at[:, row_at, 0], ids.at[pl.ds(n_panel, n_rows)], sems.at[1]),
        pltpu.make_async_copy(col_ids.at[:, col_at, 0], ids.at[pl.ds(n_panel + n_rows, n_cols)], sems.at[2]),
    ]
    for copy in copies:
        copy.start()
    piece_copies, inverse_copies = start_load(teacher, inverse, inverse_ref, pieces, piece_sems, inverse_sems)
    widen(piece_copies, pieces, left, right)
    for copy in inverse_copies:
        copy.start()
    for copy in copies:
        copy.wait()
    width = panel_out.shape[0]

    take = functools.partial(gather_blocks, ids, (left, right), (stage_left, stage_right))
    slots = stage_left.shape[0]
    take(lambda i, b: n_panel + 2 * slots * i + 4 * (b // 2) + b % 2 + 2 * (col_at % 2), n_rows // 2, half_out, width)
    take(lambda i, b: slots * i + b, n_panel, panel_out, 0)
    take(lambda i, b: n_panel + n_rows + slots * i + b, n_cols, col_out, 0)
    norms[...] = row_norms(half_out[:, width:], scale)
    for at in range(0, width, WIDE):
        norm_out[:, at : at + WIDE] = lane_norms(panel_out[at : at + WIDE, :], scale)
    for copy in inverse_copies:
        copy.wait()
    cross_rows(scale, lambda: half_out[:, width:], norms, panel_out, norm_out, cross)
    for j in range(width // WIDE):
        factor_columns(j, inverse_ref, cross, half_out)


def cross_rows(scale, rows, norms, panel_ref, norm_ref, cross):
    for at in range(0, panel_ref.shape[0], WIDE):
        to = slice(at, at + WIDE)
        cross[:, to] = gauss(scale, nt_dot(rows(), panel_ref[to, :]), norms[...], norm_ref[:1, to]).astype(BF16)


def factor_columns(j, inverse_ref, cross, factor_ref):
    to, depth = slice(j * WIDE, (j + 1) * WIDE), (j + 1) * WIDE
    factor_ref[:, to] = nt_dot(cross[:, :depth], inverse_ref[to, :depth]).astype(BF16)


def column_kernel(scale, n_row, n_col, stretch, col_ref, panel_ref, norm_ref, inverse_ref, mine, mine_norms,
                  factor_out, col_norms, first_out, norms, cross):
    norms[...] = row_norms(col_ref[...], scale)
    for at in range(0, col_ref.shape[0], WIDE):
        col_norms[:, at : at + WIDE] = lane_norms(col_ref[at : at + WIDE, :], scale)
    cross_rows(scale, lambda: col_ref[...], norms, panel_ref, norm_ref, cross)
    for j in range(panel_ref.shape[0] // WIDE):
        factor_columns(j, inverse_ref, cross, factor_out)
    step = mine.shape[0] // (2 * stretch) - 1
    assert blocks_reached(step, n_row, n_col) == n_row
    update_tile(scale, n_row, n_col, stretch, step, lax.axis_index("col") % 2, mine, mine_norms,
                factor_out, col_ref, col_norms, first_out)


def blocks_reached(step, n_row, n_col):
    blocks = min(n_row, ((4 * step + 3) * n_row + n_row - 1) // n_col + 1)
    return -(-blocks * LANES // WIDE) * (WIDE // LANES)


def update_tile(scale, n_row, n_col, stretch, step, pair, half, row_norm, factor_ref, col_ref, norms, stage):
    row_at, col_at = lax.axis_index("row"), lax.axis_index("col")
    width, tile = factor_ref.shape[1], 2 * stretch
    here = slice(step * tile, (step + 1) * tile)
    first_row = ((4 * step + 2 * pair) * n_row + row_at) * stretch
    above = lax.broadcasted_iota(jnp.int32, (tile, LANES), 0)
    above = above // stretch * (n_row * stretch) + above % stretch - lax.broadcasted_iota(jnp.int32, (tile, LANES), 1)
    blocks = blocks_reached(step, n_row, n_col)
    for at in range(0, blocks * LANES, WIDE):
        to = slice(at, at + WIDE)
        update = nt_dot(half[here, :width], factor_ref[to, :])
        inner = nt_dot(half[here, width:], col_ref[to, :])
        result = gauss(scale, inner, row_norm[here, :], norms[:1, to]) - update
        for b in range(WIDE // LANES):
            block = at // LANES + b
            first_col = (block * n_col + col_at) * stretch
            piece = result[:, b * LANES : (b + 1) * LANES]
            piece = jnp.where(above >= first_col - first_row, piece, 0.0)
            stage[pl.ds(block, tile, stride=n_row), :] = piece


def update_kernel(scale, n_row, n_col, stretch, mine, other, factor_ref, col_ref, mine_norms, norms, first,
                  out_hbm, own_out, stage, other_norms, out_sems, own_sem):
    parity = lax.axis_index("col") % 2
    width = factor_ref.shape[1]
    size = first.shape[0]
    own = pl.ds(pl.multiple_of(lax.axis_index("row") * stretch, stretch), stretch)
    puts = []

    def put(step, pair, ref):
        at = (4 * step + 2 * pair) * (stretch * n_row)
        to = pl.ds(pl.multiple_of(at, stretch * n_row), size)
        puts.append(pltpu.make_async_copy(ref, out_hbm.at[to], out_sems.at[len(puts)]))
        puts[-1].start()

    steps = mine.shape[0] // (2 * stretch)
    put(steps - 1, parity, first)
    own_copy = pltpu.make_async_copy(factor_ref.at[own], own_out, own_sem)
    own_copy.start()
    for step in range(steps):
        for slot in range(2 * (steps - 1 - step) - 1, 2 * (steps - 1 - step) + 1):
            for block in range(blocks_reached(step, n_row, n_col), n_row):
                stage[slot, pl.ds(block, 2 * stretch, stride=n_row), :] = jnp.zeros((2 * stretch, LANES), F32)
    other_norms[...] = row_norms(other[:, width:], scale)
    for step in range(steps)[::-1]:
        for pair, half, row_norm in ((parity, mine, mine_norms), (1 - parity, other, other_norms)):
            if step == steps - 1 and half is mine:
                continue
            slot = stage.at[len(puts) - 1]
            update_tile(scale, n_row, n_col, stretch, step, pair, half, row_norm, factor_ref, col_ref, norms, slot)
            put(step, pair, slot)
    own_copy.wait()
    for copy in puts:
        copy.wait()


def shards(teacher, panel_ids, rest_ids, inverse):
    n_row, n_col = lax.axis_size("row"), lax.axis_size("col")
    stretch = rest_ids.shape[2]
    width = inverse.shape[0]
    emb = teacher.shape[1]
    n_rows, n_cols = n_col * stretch, n_row * stretch
    half = n_rows // 2
    scale = 2.0 / emb * math.log2(math.e)
    vmem = pl.BlockSpec(memory_space=pltpu.VMEM)
    hbm = pl.BlockSpec(memory_space=pl.ANY)
    near = functools.partial(pltpu.with_memory_space_constraint, memory_space=pltpu.VMEM)
    far = functools.partial(pltpu.with_memory_space_constraint, memory_space=pltpu.HBM)
    wide = (n_row * n_col, 2, 1, stretch)
    which = lax.iota(jnp.int32, math.prod(wide)).reshape(wide) // stretch % 2
    both = jnp.where(which == 0, rest_ids.reshape(1, 1, 1, -1), panel_ids.reshape(1, 1, 1, -1))
    both = lax.all_to_all(both, ("row", "col"), 0, 0, tiled=True)

    n_table = teacher.shape[0]
    mine, panel_emb, panel_norms, col_emb, inverse_near, mine_norms = pl.pallas_call(
        functools.partial(rows_kernel, scale, (n_col, n_col, n_row)),
        out_shape=(
            pltpu.VMEM((half, width + emb), BF16),
            pltpu.VMEM((width, emb), BF16),
            pltpu.VMEM((8, width), F32),
            pltpu.VMEM((n_cols, emb), BF16),
            pltpu.VMEM((width, width), BF16),
            pltpu.VMEM((half, LANES), F32),
        ),
        in_specs=[hbm] * 5,
        out_specs=[vmem] * 6,
        scratch_shapes=[
            pltpu.VMEM((n_table // PIECE, PIECE, emb), BF16),
            pltpu.VMEM((n_table, LANES), F32),
            pltpu.VMEM((n_table, LANES), F32),
            pltpu.VMEM((8, stretch, LANES), F32),
            pltpu.VMEM((8, stretch, LANES), F32),
            pltpu.VMEM((half, width), BF16),
            pltpu.SMEM((2 * n_col + n_row, 1, stretch), jnp.int32),
            pltpu.SemaphoreType.DMA((3,)),
            pltpu.SemaphoreType.DMA((n_table // PIECE,)),
            pltpu.SemaphoreType.DMA((width // WIDE,)),
        ],
        compiler_params=pltpu.CompilerParams(vmem_limit_bytes=36 * MIB),
        name="rows",
    )(far(teacher), far(inverse), both, both.reshape(n_col, n_row, 2, 1, stretch),
      both.reshape(n_row, n_col, 2, 1, stretch))

    other = lax.ppermute(mine, "col", [(i, i ^ 1) for i in range(n_col)])

    size = 2 * stretch * n_row
    factors, col_norms, first = pl.pallas_call(
        functools.partial(column_kernel, scale, n_row, n_col, stretch),
        out_shape=(
            pltpu.VMEM((n_cols, width), BF16),
            pltpu.VMEM((8, n_cols), F32),
            pltpu.VMEM((size, stretch), F32),
        ),
        in_specs=[vmem] * 6,
        out_specs=[vmem] * 3,
        scratch_shapes=[
            pltpu.VMEM((n_cols, LANES), F32),
            pltpu.VMEM((n_cols, width), BF16),
        ],
        compiler_params=pltpu.CompilerParams(vmem_limit_bytes=14 * MIB),
        cost_estimate=pl.CostEstimate(
            flops=2 * n_cols * width * width, bytes_accessed=16 * MIB, transcendentals=n_cols * width),
        name="columns",
    )(near(col_emb), near(panel_emb), near(panel_norms), near(inverse_near), near(mine), near(mine_norms))

    trailing, own = pl.pallas_call(
        functools.partial(update_kernel, scale, n_row, n_col, stretch),
        out_shape=(
            jax.ShapeDtypeStruct((n_rows * n_row, stretch), F32),
            jax.ShapeDtypeStruct((stretch, width), BF16),
        ),
        in_specs=[vmem] * 7,
        out_specs=[hbm] * 2,
        scratch_shapes=[
            pltpu.VMEM((n_col // 2 - 1, size, stretch), F32),
            pltpu.VMEM((half, LANES), F32),
            pltpu.SemaphoreType.DMA((n_col // 2,)),
            pltpu.SemaphoreType.DMA,
        ],
        compiler_params=pltpu.CompilerParams(vmem_limit_bytes=20 * MIB),
        name="update",
    )(near(mine), near(other), near(factors), near(col_emb), near(mine_norms), near(col_norms), near(first))
    return (
        trailing.reshape(n_col, 1, stretch, n_row, 1, stretch),
        own.reshape(1, 1, stretch, width),
    )


def solution(mesh):
    return jax.shard_map(
        shards,
        mesh=mesh,
        in_specs=(P(), P("col"), P("row", "col", None), P()),
        out_specs=(P(None, "row", None, None, "col", None), P("row", "col", None, None)),
        check_vma=False,
    )
```
